32 devices in a mesh: section: 2 (over core), seq: 4 (over z), cfg: 4 (over y, x).
Axes of the slice: x: 2, y: 2, z: 4, core: 2. Of those that a mesh axis runs over, the one named last changes fastest.
Arguments:
- hidden_states: bfloat16 [4, 4, 64, 3072], P('cfg', None, 'seq'), may hold values from -250 to 250
- latent: float32 [2, 4, 64, 64], P('section', None, 'seq'), may hold values from -6 to 6
- stale_cache: bfloat16 [2, 4, 4, 256, 128], P('section', 'cfg', 'seq'), may hold values from -140 to 140
- qkv_weight: bfloat16 [2, 3072, 3, 256], P('section', None, None, 'cfg'), may hold values from -0.109375 to 0.109375
- out_weight: bfloat16 [2, 3072, 256], P('section', 'seq', 'cfg'), may hold values from -0.375 to 0.375
- modulation: float32 [2, 6, 3072], P('section'), may hold values from -2.5 to 2.5
- out_modulation: float32 [2, 3072], replicated, may hold values from -2.5 to 2.5
- proj_weight: bfloat16 [3072, 64], replicated, may hold values from -0.109375 to 0.109375
- solver_coef: float32 [2, 3], P('section'), may hold values from 0.5 to 2
- video_len: int32 [2], replicated, may hold values from 15 to 30, as said below
- text_len: int32 [4], replicated, may hold values from 1 to 226, as said below
- positions: int32 [3, 2, 4, 64], P(None, None, None, 'seq'), may hold values from 0 to 47
Outputs:
- new_latent: float32 [2, 4, 64, 64], P('section', None, 'seq')
- new_cache: bfloat16 [2, 4, 4, 256, 128], P('section', 'cfg', 'seq')
The draws below stay inside these ranges and needn't reach their ends.
Inputs may be any that keep to these rules, and one draw needn't show every extreme that they name: `video_len`: in every draw one request has exactly 30 video tokens. `text_len`: in every draw some sequence has all 226 text tokens live.
All inputs are finite; a program needn't handle non-finite values.
Results may differ from the reference program's by a relative error of at most 0.02.
Values may be sent and summed in bfloat16 or wider, within the bound.
A program may use at most 128 MiB of HBM per device.

```python
import math
import jax
import jax.numpy as jnp
from jax import lax

D = 3072
HD = 64
TEXT = 226
OUT = 64
PATCHES = 4
REQS = 2
SEQS = 4
SECTIONS = 2
PATCH_LEN = 64
SEQ = 256
HEADS = 4
ATT = 256
GROUPS = 4
PAIRS = 4
N_SEQ = 4
N_CFG = 4


def draw_hidden_states(key, part):
    subkeys = jax.random.split(key, 1)
    shape = (SEQS, PATCHES, PATCH_LEN, D)
    values = jnp.clip(jax.random.normal(subkeys[0], shape, jnp.float32), -6.0, 6.0) * 0.2
    return values.astype(jnp.bfloat16)


def draw_stale_cache(key, part):
    subkeys = jax.random.split(key, 1)
    shape = (SECTIONS, GROUPS, PAIRS, SEQ, 2 * HD)
    values = jnp.clip(jax.random.normal(subkeys[0], shape, jnp.float32), -6.0, 6.0)
    return values.astype(jnp.bfloat16)


def draw_video_len(key, part):
    subkeys = jax.random.split(key, 2)
    longest = SEQ - TEXT
    others = jax.random.randint(subkeys[0], (REQS,), longest // 2, longest + 1)
    which_one = jax.random.randint(subkeys[1], (), 0, REQS)
    return jnp.where(jnp.arange(REQS) == which_one, longest, others).astype(jnp.int32)


def draw_text_len(key, part):
    subkeys = jax.random.split(key, 2)
    others = jax.random.randint(subkeys[0], (SEQS,), 1, TEXT + 1)
    which_one = jax.random.randint(subkeys[1], (), 0, SEQS)
    return jnp.where(jnp.arange(SEQS) == which_one, TEXT, others).astype(jnp.int32)


def place_ends(result, rng, least, high):
    longest = result.shape.index(max(result.shape))
    spots = []
    for shift in (0, 1):
        where = [jax.random.randint(jax.random.fold_in(rng, axis), (), 0, length) for axis, length in enumerate(result.shape)]
        where[longest] = (where[longest] + shift) % result.shape[longest]
        spots.append(tuple(where))
    return result.at[spots[0]].set(least).at[spots[1]].set(high)


def block_scale(key, shape, pieces, low, largest):
    level = 1.0
    for axis_at, blocks in pieces:
        draws = jax.random.uniform(jax.random.fold_in(jax.random.fold_in(key, 6), axis_at), (blocks,), jnp.float32, low / len(pieces), largest / len(pieces))
        level = level * jnp.repeat(jnp.exp(draws), shape[axis_at] // blocks).reshape((-1,) + (1,) * (len(shape) - 1 - axis_at))
    return level


def gaussian(stream_key, shape, width, reach, shards=(), held_as=jnp.bfloat16):
    entries = jax.random.normal(stream_key, shape, jnp.float32) * width
    if len(shards) > 0:
        entries = block_scale(stream_key, shape, shards, -0.22, 0.18) * entries
    return jnp.clip(entries, min=-reach, max=reach).astype(held_as)


def setup_inputs(seed: int = 0) -> dict:
    key_of = jax.random.split(jax.random.key(seed), 13)
    hidden_states = draw_hidden_states(jax.random.fold_in(key_of[12], 71), 0)
    latent = gaussian(key_of[1], (REQS, PATCHES, PATCH_LEN, OUT), 1.0, 6.0, ((0, 2), (2, 4)), jnp.float32)
    stale_cache = draw_stale_cache(jax.random.fold_in(key_of[12], 71), 0)
    qkv_weight = gaussian(key_of[3], (SECTIONS, D, 3, ATT), D ** -0.5, 0.109375, ((0, 2), (3, 4)))
    out_weight = gaussian(key_of[4], (SECTIONS, D, ATT), ATT ** -0.5, 0.375, ((0, 2), (1, 4), (2, 4)))
    modulation = gaussian(key_of[5], (SECTIONS, 6, D), 0.5, 2.5, ((0, 2),), jnp.float32)
    out_modulation = gaussian(key_of[6], (2, D), 0.5, 2.5, (), jnp.float32)
    proj_weight = gaussian(key_of[7], (D, OUT), D ** -0.5, 0.109375)
    solver_coef = jnp.clip(0.5 + 1.5 * jax.random.uniform(key_of[8], (REQS, 3), jnp.float32) ** block_scale(key_of[8], (REQS, 3), ((0, 2),), -0.2, 0.2), 0.5, 2.0)
    video_len = draw_video_len(jax.random.fold_in(key_of[12], 71), 0)
    text_len = draw_text_len(jax.random.fold_in(key_of[12], 71), 0)
    positions = place_ends(jax.random.randint(key_of[11], (3, REQS, PATCHES, PATCH_LEN), 0, 48), jax.random.fold_in(key_of[11], 1), 0, 47).astype(jnp.int32)
    return dict(hidden_states=hidden_states, latent=latent, stale_cache=stale_cache, qkv_weight=qkv_weight, out_weight=out_weight, modulation=modulation, out_modulation=out_modulation, proj_weight=proj_weight, solver_coef=solver_coef, video_len=video_len, text_len=text_len, positions=positions)


def row_norm(values):
    centered = values - lax.optimization_barrier(jnp.mean(values, axis=-1, keepdims=True))
    return centered * lax.rsqrt(lax.optimization_barrier(jnp.mean(centered * centered, axis=-1, keepdims=True)) + 1e-05)

def head_norm(values):
    centered = values - lax.optimization_barrier(jnp.mean(values, axis=-1, keepdims=True))
    return centered * lax.rsqrt(lax.optimization_barrier(jnp.mean(centered * centered, axis=-1, keepdims=True)) + 1e-06)

def rope_angles(places, head_size):
    half_size = head_size // 2
    pairs_t = head_size // 8
    pairs_h = (half_size - pairs_t) // 2
    pair_index = jnp.arange(half_size)
    first_part = pair_index < pairs_t
    second_part = jnp.logical_and(pair_index >= pairs_t, pair_index < pairs_t + pairs_h)
    third_part = pair_index >= pairs_t + pairs_h
    local_index = jnp.where(first_part, pair_index, jnp.where(second_part, pair_index - pairs_t, pair_index - pairs_t - pairs_h))
    axis_span = jnp.where(first_part, 2 * pairs_t, 2 * pairs_h)
    frequency = jnp.exp(-math.log(10000.0) * 2.0 * local_index.astype(jnp.float32) / axis_span.astype(jnp.float32))
    angles = places[0][..., None] * first_part.astype(jnp.float32)
    angles = angles + places[1][..., None] * second_part.astype(jnp.float32)
    angles = angles + places[2][..., None] * third_part.astype(jnp.float32)
    return angles * frequency

def rotate(values, cos_table, sin_table):
    half_size = values.shape[-1] // 2
    first_half = values[..., :half_size]
    second_half = values[..., half_size:]
    return jnp.concatenate([first_half * cos_table - second_half * sin_table, second_half * cos_table + first_half * sin_table], axis=-1)

def attend_pair(work_item):
    fresh_one, stale_one, query_one, live_one = work_item
    key_patch = jnp.arange(SEQ) // PATCH_LEN
    outputs = []
    for patch_id in range(PATCHES):
        key_rows = jnp.where((key_patch <= patch_id)[:, None], fresh_one, stale_one)
        query_block = query_one[patch_id * PATCH_LEN:(patch_id + 1) * PATCH_LEN]
        scores = jnp.dot(query_block, key_rows[:, :HD].T, preferred_element_type=jnp.float32) * HD ** (-0.5)
        scores = jnp.where(live_one[None, :], scores, -jnp.inf)
        row_max = lax.optimization_barrier(jnp.max(scores, axis=1, keepdims=True))
        weights = jnp.exp(scores - row_max)
        row_sum = lax.optimization_barrier(jnp.sum(weights, axis=1, keepdims=True))
        combined = jnp.dot(weights.astype(jnp.bfloat16), key_rows[:, HD:], preferred_element_type=jnp.float32)
        outputs.append((combined / row_sum).astype(jnp.bfloat16))
    return jnp.concatenate(outputs, axis=0)

def reference(hidden_states, latent, stale_cache, qkv_weight, out_weight, modulation, out_modulation, proj_weight, solver_coef, video_len, text_len, positions):
    row_ids = jnp.arange(SEQ)
    text_rows = row_ids < TEXT
    video_rep = jnp.repeat(video_len, 2)
    live_keys = jnp.where(text_rows[None, :], row_ids[None, :] < text_len[:, None], row_ids[None, :] - TEXT < video_rep[:, None])
    places = positions.reshape(3, REQS, SEQ).astype(jnp.float32)
    angles = rope_angles(places, HD)
    angles = jnp.where(text_rows[None, :, None], 0.0, angles)
    angles = jnp.repeat(angles, 2, axis=0)
    cos_table = jnp.cos(angles)[:, :, None, :]
    sin_table = jnp.sin(angles)[:, :, None, :]
    group_heads = HEADS // N_CFG
    hidden = hidden_states.reshape(SEQS, SEQ, D)
    caches = []
    for section_id in range(SECTIONS):
        mod_rows = modulation[section_id]
        normed = row_norm(hidden.astype(jnp.float32))
        shift_rows = jnp.where(text_rows[:, None], mod_rows[3], mod_rows[0])
        scale_rows = jnp.where(text_rows[:, None], mod_rows[4], mod_rows[1])
        gate_rows = jnp.where(text_rows[:, None], mod_rows[5], mod_rows[2])
        mixed_rows = (normed * (1.0 + scale_rows) + shift_rows).astype(jnp.bfloat16)
        projected = jnp.dot(mixed_rows.reshape(SEQS * SEQ, D), qkv_weight[section_id].reshape(D, 3 * ATT), preferred_element_type=jnp.float32)
        projected = projected.reshape(SEQS, SEQ, 3, HEADS, HD)
        queries = rotate(head_norm(projected[:, :, 0]), cos_table, sin_table).astype(jnp.bfloat16)
        key_part = rotate(head_norm(projected[:, :, 1]), cos_table, sin_table).astype(jnp.bfloat16)
        value_part = projected[:, :, 2].astype(jnp.bfloat16)
        fresh_rows = jnp.concatenate([key_part, value_part], axis=-1).transpose(0, 2, 1, 3)
        stale_rows = stale_cache[section_id].reshape(N_CFG, SEQS, group_heads, SEQ, 2 * HD).transpose(1, 0, 2, 3, 4).reshape(SEQS, HEADS, SEQ, 2 * HD)
        query_rows = queries.transpose(0, 2, 1, 3).reshape(SEQS * HEADS, SEQ, HD)
        live_rep = jnp.repeat(live_keys, HEADS, axis=0)
        attended = lax.map(attend_pair, (fresh_rows.reshape(SEQS * HEADS, SEQ, 2 * HD), stale_rows.reshape(SEQS * HEADS, SEQ, 2 * HD), query_rows, live_rep))
        attended = attended.reshape(SEQS, HEADS, SEQ, HD).transpose(0, 2, 1, 3).reshape(SEQS * SEQ, ATT)
        update = jnp.dot(attended, out_weight[section_id].T, preferred_element_type=jnp.float32).reshape(SEQS, SEQ, D)
        hidden = (hidden.astype(jnp.float32) + gate_rows * update).astype(jnp.bfloat16)
        caches.append(fresh_rows.reshape(SEQS, N_CFG, group_heads, SEQ, 2 * HD).transpose(1, 0, 2, 3, 4).reshape(N_CFG, N_SEQ, SEQ, 2 * HD))
    normed = row_norm(hidden.astype(jnp.float32))
    normed_out = (normed * (1.0 + out_modulation[1]) + out_modulation[0]).astype(jnp.bfloat16)
    predicted = jnp.dot(normed_out.reshape(SEQS * SEQ, D), proj_weight, preferred_element_type=jnp.float32).reshape(REQS, 2, SEQ, OUT)
    guide_scale = solver_coef[:, 2][:, None, None]
    guided = predicted[:, 0] + guide_scale * (predicted[:, 1] - predicted[:, 0])
    latent_rows = latent.reshape(REQS, SEQ, OUT)
    new_latent = solver_coef[:, 0][:, None, None] * latent_rows + solver_coef[:, 1][:, None, None] * guided
    return (new_latent.reshape(REQS, PATCHES, PATCH_LEN, OUT), jnp.stack(caches, axis=0))
```

```python
import math

import jax
import jax.numpy as jnp
from jax import lax
from jax.sharding import PartitionSpec as P

HD = 64
TEXT = 226


def from_behind(value, axis, steps):
    count = lax.axis_size(axis)
    pairs = [(source, (source + steps) % count) for source in range(count)]
    return lax.ppermute(value, axis, pairs)


def row_norm(values):
    centered = values - jnp.mean(values, axis=-1, keepdims=True)
    return centered * lax.rsqrt(jnp.mean(centered * centered, axis=-1, keepdims=True) + 1e-05)


def head_norm(values):
    centered = values - jnp.mean(values, axis=-1, keepdims=True)
    return centered * lax.rsqrt(jnp.mean(centered * centered, axis=-1, keepdims=True) + 1e-06)


def rope_angles(places, head_size):
    half_size = head_size // 2
    pairs_t = head_size // 8
    pairs_h = (half_size - pairs_t) // 2
    pair_index = jnp.arange(half_size)
    first_part = pair_index < pairs_t
    second_part = jnp.logical_and(pair_index >= pairs_t, pair_index < pairs_t + pairs_h)
    third_part = pair_index >= pairs_t + pairs_h
    local_index = jnp.where(
        first_part,
        pair_index,
        jnp.where(second_part, pair_index - pairs_t, pair_index - pairs_t - pairs_h),
    )
    axis_span = jnp.where(first_part, 2 * pairs_t, 2 * pairs_h)
    frequency = jnp.exp(
        -math.log(10000.0) * 2.0 * local_index.astype(jnp.float32) / axis_span.astype(jnp.float32)
    )
    angles = places[0][..., None] * first_part.astype(jnp.float32)
    angles = angles + places[1][..., None] * second_part.astype(jnp.float32)
    angles = angles + places[2][..., None] * third_part.astype(jnp.float32)
    return angles * frequency


def rotate(values, cos_table, sin_table):
    half_size = values.shape[-1] // 2
    first_half = values[..., :half_size]
    second_half = values[..., half_size:]
    return jnp.concatenate(
        [
            first_half * cos_table - second_half * sin_table,
            second_half * cos_table + first_half * sin_table,
        ],
        axis=-1,
    )


def spread(values):
    return lax.all_gather(values, "cfg", axis=0, tiled=True)


def handoff(values):
    return from_behind(values, "section", 1)


def per_device(
    hidden_states,
    latent,
    stale_cache,
    qkv_weight,
    out_weight,
    modulation,
    out_modulation,
    proj_weight,
    solver_coef,
    video_len,
    text_len,
    positions,
):
    section_id = lax.axis_index("section")
    shard_id = lax.axis_index("seq")
    seq_devices = lax.axis_size("seq")
    patches = hidden_states.shape[1]
    patch_dev = hidden_states.shape[2]
    width = hidden_states.shape[3]
    patch_len = patch_dev * seq_devices
    total_len = patch_len * patches
    group_heads = qkv_weight.shape[3] // HD
    qkv_full = qkv_weight[0].reshape(width, 3, group_heads, HD)
    out_full = lax.all_gather(out_weight[0], "seq", axis=0, tiled=True).reshape(
        width, group_heads, HD
    )
    mod_rows = modulation[0]
    stale_rows = stale_cache[0, 0, 0]
    my_sequence = shard_id // group_heads
    row_ids = jnp.arange(total_len)
    text_limit = lax.dynamic_index_in_dim(text_len, my_sequence, keepdims=False)
    video_limit = lax.dynamic_index_in_dim(video_len, my_sequence // 2, keepdims=False)
    live_keys = jnp.where(row_ids < TEXT, row_ids < text_limit, row_ids - TEXT < video_limit)
    key_patch = row_ids // patch_len
    query_block = patch_len
    while query_block > 1024 and query_block % 2 == 0:
        query_block = query_block // 2
    scale_factor = HD ** (-0.5)
    key_cache = stale_rows
    received = hidden_states
    first_patch = 0
    for tick_id in range(2):
        hidden = jnp.where(section_id == 0, hidden_states, received)
        run_key_cache = stale_rows
        patch_count = hidden.shape[1]
        row_place = (
            (first_patch + jnp.arange(patch_count))[:, None] * patch_len
            + shard_id * patch_dev
            + jnp.arange(patch_dev)[None, :]
        )
        text_rows = (row_place < TEXT)[:, :, None]
        run_normed = row_norm(hidden.astype(jnp.float32))
        shift_rows = jnp.where(text_rows, mod_rows[3], mod_rows[0])
        scale_rows = jnp.where(text_rows, mod_rows[4], mod_rows[1])
        gate_rows = jnp.where(text_rows, mod_rows[5], mod_rows[2])
        mixed_rows = (run_normed * (1.0 + scale_rows) + shift_rows).astype(jnp.bfloat16)
        mixed_rows = spread(mixed_rows)
        seq_count = mixed_rows.shape[0]
        projected = jnp.einsum(
            "spqd,djge->sgjpqe", mixed_rows, qkv_full, preferred_element_type=jnp.float32
        )
        places = lax.dynamic_slice_in_dim(positions, first_patch, patch_count, 2).astype(
            jnp.float32
        )
        angles = rope_angles(places, HD)
        angles = jnp.where(text_rows[None], 0.0, angles)
        angles = jnp.repeat(angles, 2, axis=0)[:, None]
        cos_table = jnp.cos(angles)
        sin_table = jnp.sin(angles)
        queries = rotate(head_norm(projected[:, :, 0]), cos_table, sin_table)
        key_part = rotate(head_norm(projected[:, :, 1]), cos_table, sin_table)
        stacked = jnp.stack([queries, key_part, projected[:, :, 2]], axis=2).astype(jnp.bfloat16)
        outgoing = stacked.reshape(seq_count * group_heads, 3, patch_count, patch_dev * HD)
        incoming = lax.all_to_all(outgoing, "seq", split_axis=0, concat_axis=3, tiled=True)
        incoming = incoming.reshape(3, patch_count * patch_len, HD)
        fresh_rows = jnp.concatenate([incoming[1], incoming[2]], axis=-1)
        run_key_cache = lax.dynamic_update_slice_in_dim(
            run_key_cache, fresh_rows, first_patch * patch_len, 0
        )
        block_count = patch_count * patch_len // query_block

        def attend(work_item):
            query_rows, block_id = work_item
            patch_now = first_patch + block_id * query_block // patch_len
            key_rows = jnp.where((key_patch <= patch_now)[:, None], run_key_cache, stale_rows)
            scores = (
                jnp.dot(query_rows, key_rows[:, :HD].T, preferred_element_type=jnp.float32)
                * scale_factor
            )
            scores = jnp.where(live_keys[None, :], scores, -jnp.inf)
            row_max = jnp.max(scores, axis=1, keepdims=True)
            weights = jnp.exp(scores - row_max)
            row_sum = jnp.sum(weights, axis=1, keepdims=True)
            combined = jnp.dot(
                weights.astype(jnp.bfloat16), key_rows[:, HD:], preferred_element_type=jnp.float32
            )
            return (combined / row_sum).astype(jnp.bfloat16)

        attended = lax.map(
            attend, (incoming[0].reshape(block_count, query_block, HD), jnp.arange(block_count))
        )
        attended = attended.reshape(patch_count, seq_devices, patch_dev * HD)[None]
        returned = lax.all_to_all(attended, "seq", split_axis=2, concat_axis=0, tiled=True)
        returned = returned.reshape(seq_count, group_heads, patch_count, patch_dev, HD)
        update = lax.psum_scatter(
            jnp.einsum("sgpqe,dge->spqd", returned, out_full, preferred_element_type=jnp.float32),
            "cfg",
            scatter_dimension=0,
            tiled=True,
        )
        result = (hidden.astype(jnp.float32) + gate_rows * update).astype(jnp.bfloat16)
        key_cache = jnp.where(section_id == tick_id, run_key_cache, key_cache)
        if tick_id == 0:
            received = handoff(result)
    normed = row_norm(result.astype(jnp.float32))
    normed_out = (normed * (1.0 + out_modulation[1]) + out_modulation[0]).astype(jnp.bfloat16)
    own_values = jnp.einsum(
        "spqd,do->spqo", normed_out, proj_weight, preferred_element_type=jnp.float32
    )
    all_values = lax.all_gather(own_values, ("section", "cfg"), axis=0, tiled=True)
    last = all_values.shape[0] // 2
    predicted = lax.dynamic_slice_in_dim(all_values, last + 2 * section_id, 2, 0)
    solver_row = solver_coef[0]
    guided = predicted[0] + solver_row[2] * (predicted[1] - predicted[0])
    new_latent = (solver_row[0] * latent[0] + solver_row[1] * guided)[None]
    return (new_latent, key_cache[None, None, None])


def solution(mesh):
    return jax.shard_map(
        per_device,
        mesh=mesh,
        in_specs=(
            P("cfg", None, "seq", None),
            P("section", None, "seq", None),
            P("section", "cfg", "seq", None, None),
            P("section", None, None, "cfg"),
            P("section", "seq", "cfg"),
            P("section", None, None),
            P(),
            P(),
            P("section", None),
            P(),
            P(),
            P(None, None, None, "seq"),
        ),
        out_specs=(P("section", None, "seq", None), P("section", "cfg", "seq", None, None)),
        check_vma=False,
    )
```

```python
import math

import jax
import jax.numpy as jnp
from jax import lax
from jax.experimental import pallas as pl
from jax.experimental.pallas import tpu as pltpu
from jax.sharding import PartitionSpec as P

HD = 64
TEXT = 226


def from_behind(value, axis, steps):
    count = lax.axis_size(axis)
    pairs = [(source, (source + steps) % count) for source in range(count)]
    return lax.ppermute(value, axis, pairs)


def row_norm(values):
    centered = values - jnp.mean(values, axis=-1, keepdims=True)
    return centered * lax.rsqrt(jnp.mean(centered * centered, axis=-1, keepdims=True) + 1e-05)


def head_norm(values):
    centered = values - jnp.mean(values, axis=-1, keepdims=True)
    return centered * lax.rsqrt(jnp.mean(centered * centered, axis=-1, keepdims=True) + 1e-06)


def rope_angles(places, head_size):
    half_size = head_size // 2
    pairs_t = head_size // 8
    pairs_h = (half_size - pairs_t) // 2
    pair_index = jnp.arange(half_size)
    first_part = pair_index < pairs_t
    second_part = jnp.logical_and(pair_index >= pairs_t, pair_index < pairs_t + pairs_h)
    third_part = pair_index >= pairs_t + pairs_h
    local_index = jnp.where(
        first_part,
        pair_index,
        jnp.where(second_part, pair_index - pairs_t, pair_index - pairs_t - pairs_h),
    )
    axis_span = jnp.where(first_part, 2 * pairs_t, 2 * pairs_h)
    frequency = jnp.exp(
        -math.log(10000.0) * 2.0 * local_index.astype(jnp.float32) / axis_span.astype(jnp.float32)
    )
    angles = places[0][..., None] * first_part.astype(jnp.float32)
    angles = angles + places[1][..., None] * second_part.astype(jnp.float32)
    angles = angles + places[2][..., None] * third_part.astype(jnp.float32)
    return angles * frequency


def rotate(values, cos_table, sin_table):
    half_size = values.shape[-1] // 2
    first_half = values[..., :half_size]
    second_half = values[..., half_size:]
    return jnp.concatenate(
        [
            first_half * cos_table - second_half * sin_table,
            second_half * cos_table + first_half * sin_table,
        ],
        axis=-1,
    )


def spread(values):
    return lax.all_gather(values, "cfg", axis=0, tiled=True)


def handoff(values):
    return from_behind(values, "section", 1)


def general(
    hidden_states,
    latent,
    stale_cache,
    qkv_weight,
    out_weight,
    modulation,
    out_modulation,
    proj_weight,
    solver_coef,
    video_len,
    text_len,
    positions,
):
    section_id = lax.axis_index("section")
    shard_id = lax.axis_index("seq")
    seq_devices = lax.axis_size("seq")
    patches = hidden_states.shape[1]
    patch_dev = hidden_states.shape[2]
    width = hidden_states.shape[3]
    patch_len = patch_dev * seq_devices
    total_len = patch_len * patches
    group_heads = qkv_weight.shape[3] // HD
    qkv_full = qkv_weight[0].reshape(width, 3, group_heads, HD)
    out_full = lax.all_gather(out_weight[0], "seq", axis=0, tiled=True).reshape(
        width, group_heads, HD
    )
    mod_rows = modulation[0]
    stale_rows = stale_cache[0, 0, 0]
    my_sequence = shard_id // group_heads
    row_ids = jnp.arange(total_len)
    text_limit = lax.dynamic_index_in_dim(text_len, my_sequence, keepdims=False)
    video_limit = lax.dynamic_index_in_dim(video_len, my_sequence // 2, keepdims=False)
    live_keys = jnp.where(row_ids < TEXT, row_ids < text_limit, row_ids - TEXT < video_limit)
    key_patch = row_ids // patch_len
    query_block = patch_len
    while query_block > 1024 and query_block % 2 == 0:
        query_block = query_block // 2
    scale_factor = HD ** (-0.5)
    key_cache = stale_rows
    received = hidden_states
    first_patch = 0
    for tick_id in range(2):
        hidden = jnp.where(section_id == 0, hidden_states, received)
        run_key_cache = stale_rows
        patch_count = hidden.shape[1]
        row_place = (
            (first_patch + jnp.arange(patch_count))[:, None] * patch_len
            + shard_id * patch_dev
            + jnp.arange(patch_dev)[None, :]
        )
        text_rows = (row_place < TEXT)[:, :, None]
        run_normed = row_norm(hidden.astype(jnp.float32))
        shift_rows = jnp.where(text_rows, mod_rows[3], mod_rows[0])
        scale_rows = jnp.where(text_rows, mod_rows[4], mod_rows[1])
        gate_rows = jnp.where(text_rows, mod_rows[5], mod_rows[2])
        mixed_rows = (run_normed * (1.0 + scale_rows) + shift_rows).astype(jnp.bfloat16)
        mixed_rows = spread(mixed_rows)
        seq_count = mixed_rows.shape[0]
        projected = jnp.einsum(
            "spqd,djge->sgjpqe", mixed_rows, qkv_full, preferred_element_type=jnp.float32
        )
        places = lax.dynamic_slice_in_dim(positions, first_patch, patch_count, 2).astype(
            jnp.float32
        )
        angles = rope_angles(places, HD)
        angles = jnp.where(text_rows[None], 0.0, angles)
        angles = jnp.repeat(angles, 2, axis=0)[:, None]
        cos_table = jnp.cos(angles)
        sin_table = jnp.sin(angles)
        queries = rotate(head_norm(projected[:, :, 0]), cos_table, sin_table)
        key_part = rotate(head_norm(projected[:, :, 1]), cos_table, sin_table)
        stacked = jnp.stack([queries, key_part, projected[:, :, 2]], axis=2).astype(jnp.bfloat16)
        outgoing = stacked.reshape(seq_count * group_heads, 3, patch_count, patch_dev * HD)
        incoming = lax.all_to_all(outgoing, "seq", split_axis=0, concat_axis=3, tiled=True)
        incoming = incoming.reshape(3, patch_count * patch_len, HD)
        fresh_rows = jnp.concatenate([incoming[1], incoming[2]], axis=-1)
        run_key_cache = lax.dynamic_update_slice_in_dim(
            run_key_cache, fresh_rows, first_patch * patch_len, 0
        )
        block_count = patch_count * patch_len // query_block

        def attend(work_item):
            query_rows, block_id = work_item
            patch_now = first_patch + block_id * query_block // patch_len
            key_rows = jnp.where((key_patch <= patch_now)[:, None], run_key_cache, stale_rows)
            scores = (
                jnp.dot(query_rows, key_rows[:, :HD].T, preferred_element_type=jnp.float32)
                * scale_factor
            )
            scores = jnp.where(live_keys[None, :], scores, -jnp.inf)
            row_max = jnp.max(scores, axis=1, keepdims=True)
            weights = jnp.exp(scores - row_max)
            row_sum = jnp.sum(weights, axis=1, keepdims=True)
            combined = jnp.dot(
                weights.astype(jnp.bfloat16), key_rows[:, HD:], preferred_element_type=jnp.float32
            )
            return (combined / row_sum).astype(jnp.bfloat16)

        attended = lax.map(
            attend, (incoming[0].reshape(block_count, query_block, HD), jnp.arange(block_count))
        )
        attended = attended.reshape(patch_count, seq_devices, patch_dev * HD)[None]
        returned = lax.all_to_all(attended, "seq", split_axis=2, concat_axis=0, tiled=True)
        returned = returned.reshape(seq_count, group_heads, patch_count, patch_dev, HD)
        update = lax.psum_scatter(
            jnp.einsum("sgpqe,dge->spqd", returned, out_full, preferred_element_type=jnp.float32),
            "cfg",
            scatter_dimension=0,
            tiled=True,
        )
        result = (hidden.astype(jnp.float32) + gate_rows * update).astype(jnp.bfloat16)
        key_cache = jnp.where(section_id == tick_id, run_key_cache, key_cache)
        if tick_id == 0:
            received = handoff(result)
    normed = row_norm(result.astype(jnp.float32))
    normed_out = (normed * (1.0 + out_modulation[1]) + out_modulation[0]).astype(jnp.bfloat16)
    own_values = jnp.einsum(
        "spqd,do->spqo", normed_out, proj_weight, preferred_element_type=jnp.float32
    )
    all_values = lax.all_gather(own_values, ("section", "cfg"), axis=0, tiled=True)
    last = all_values.shape[0] // 2
    predicted = lax.dynamic_slice_in_dim(all_values, last + 2 * section_id, 2, 0)
    solver_row = solver_coef[0]
    guided = predicted[0] + solver_row[2] * (predicted[1] - predicted[0])
    new_latent = (solver_row[0] * latent[0] + solver_row[1] * guided)[None]
    return (new_latent, key_cache[None, None, None])


def fused_kernel(
    hid, lat, stale, wqkv, wout, mod, omod, proj, coef, cos_t, sin_t, bias,
    lat_out, cache_out,
    x_buf, mix, qkv_out, qkv_in, att_out, att_in, wo, mod0, fin, pred, pred_in,
    g_s, g_r, q_s, q_r, a_s, a_r, w_s, w_r, f_s, f_r, m_s, m_r, p_s, p_r, go,
):
    sec = lax.axis_index("section")
    z = lax.axis_index("seq")
    c = lax.axis_index("cfg")
    width = hid.shape[1]
    shard = wout.shape[1]
    count = 4

    def place(section, seq, cfg):
        return {"section": section, "seq": seq, "cfg": cfg}

    def remote(src, dst, send, recv, target):
        return pltpu.make_async_remote_copy(
            src_ref=src, dst_ref=dst, send_sem=send, recv_sem=recv,
            device_id=target, device_id_type=pl.DeviceIdType.MESH,
        )

    def landed(dst, sem):
        pltpu.make_async_copy(dst, dst, sem).wait()

    barrier = pltpu.get_barrier_semaphore()
    everyone = 2 * count * count
    me = (sec * count + z) * count + c

    def greet(i, carry):
        other = lax.rem(me + i, everyone)
        pl.semaphore_signal(
            barrier, inc=1,
            device_id=place(other // 16, lax.rem(other // 4, 4), lax.rem(other, 4)),
            device_id_type=pl.DeviceIdType.MESH,
        )
        return carry

    lax.fori_loop(1, everyone, greet, 0)
    pl.semaphore_wait(barrier, everyone - 1)

    own_cols = pl.ds(pl.multiple_of(z * shard, 128), shard)

    def shard_copy(layer, k):
        return remote(
            wout, wo.at[layer, c, :, own_cols], w_s.at[k], w_r.at[layer, z],
            place(1, lax.rem(z + k, 4), c),
        )

    def forward(layer, k):
        return remote(
            wo.at[layer, c], wo.at[layer, c], f_s.at[layer, k - 1], f_r.at[layer, k - 1],
            place(1, z, lax.rem(c + k, 4)),
        )

    def shards_landed(layer):
        for zz in range(count):
            dst = wo.at[layer, c, :, zz * shard : (zz + 1) * shard]
            if layer == 0:
                landed(dst, w_r.at[layer, zz])
            else:
                @pl.when(z != zz)
                def _():
                    landed(dst, w_r.at[layer, zz])

    def forwards_landed(layer):
        for k in range(1, count):
            landed(wo.at[layer, lax.rem(c + 4 - k, 4)], f_r.at[layer, k - 1])

    def text_mask(start, rows):
        i = lax.broadcasted_iota(jnp.int32, (rows, 1), 0) + start
        return (i // 16) * 64 + z * 16 + i % 16 < TEXT

    def norm16(values):
        values = values.astype(jnp.float32)
        centered = values - jnp.mean(values, axis=-1, keepdims=True)
        return centered * lax.rsqrt(jnp.mean(centered * centered, axis=-1, keepdims=True) + 1e-05)

    def out_projection(layer, prev, gates):
        for h in range(count):
            landed(att_in.at[layer, h], a_r.at[layer, h])
        rows = [att_in[layer, h].reshape(64, 128)[:, HD:] for h in range(count)]
        joined = jnp.concatenate(rows, axis=1)
        text = text_mask(0, 64)
        for part in range(4):
            cols = slice(part * (width // 4), (part + 1) * (width // 4))
            weight = wo[layer, :, :, cols].reshape(4 * HD, width // 4)
            update = jnp.dot(joined, weight, preferred_element_type=jnp.float32)
            gate = jnp.where(text, gates[5:6, cols], gates[2:3, cols])
            x_buf[:, cols] = (prev[:, cols].astype(jnp.float32) + gate * update).astype(jnp.bfloat16)

    mod_copy = remote(mod, mod0, m_s, m_r, place(1, z, c))

    @pl.when(sec == 0)
    def _():
        mod_copy.start()
        for k in range(count):
            shard_copy(0, k).start()
        x_buf[...] = hid[...]

    @pl.when(sec == 1)
    def _():
        for k in range(1, count):
            shard_copy(1, k).start()
        wo[1, c, :, own_cols] = wout[...]
        shards_landed(0)
        pl.semaphore_wait(go, 1)
        for k in range(1, count):
            forward(0, k).start()
        shards_landed(1)
        mod_copy.wait_recv()
        forwards_landed(0)
        out_projection(0, hid, mod0)

    def mix_rows(p, carry):
        rows = pl.ds(pl.multiple_of(p * 16, 16), 16)
        text = text_mask(p * 16, 16)
        normed = norm16(x_buf[rows, :])
        scale = jnp.where(text, mod[4:5, :], mod[1:2, :])
        shift = jnp.where(text, mod[3:4, :], mod[0:1, :])
        mix[c, rows, :] = (normed * (1.0 + scale) + shift).astype(jnp.bfloat16)
        return carry

    lax.fori_loop(0, 4, mix_rows, 0)

    def gather(k):
        return remote(
            mix.at[c], mix.at[c], g_s.at[k - 1], g_r.at[k - 1], place(sec, z, lax.rem(c + k, 4))
        )

    for k in range(1, count):
        gather(k).start()

    lane = lax.broadcasted_iota(jnp.int32, (1, 128), 1)
    head = lane < HD
    low = (lane // 32) % 2 == 0

    def prepare(values, cos_table, sin_table):
        mean = jnp.sum(jnp.where(head, values, 0.0), axis=-1, keepdims=True) * (1.0 / HD)
        centered = values - mean
        square = jnp.where(head, centered * centered, 0.0)
        scale = lax.rsqrt(jnp.sum(square, axis=-1, keepdims=True) * (1.0 / HD) + 1e-06)
        normed = jnp.where(head, centered * scale, values)
        swapped = jnp.where(low, pltpu.roll(normed, 96, 1), pltpu.roll(normed, 32, 1))
        return (normed * cos_table + swapped * sin_table).astype(jnp.bfloat16).reshape(4, 16, 128)

    def qkv_copy(s):
        return remote(
            qkv_out.at[s], qkv_in.at[:, z], q_s.at[s], q_r.at[z], place(sec, s, c)
        )

    for k in range(count):
        s = lax.rem(c + 4 - k, 4)
        if k > 0:
            landed(mix.at[s], g_r.at[k - 1])
        projected = jnp.dot(mix[s], wqkv[...], preferred_element_type=jnp.float32)
        cos_table = cos_t[s // 2]
        sin_table = sin_t[s // 2]
        kv = prepare(projected[:, :128], cos_table, sin_table)
        qq = prepare(projected[:, 128:], cos_table, sin_table)

        qkv_out[s, :, :, :128] = kv
        qkv_out[s, :, :, 128:] = qq

        @pl.when(s != z)
        def _():
            qkv_copy(s).start()

    @pl.when(sec == 0)
    def _():
        pl.semaphore_signal(
            go, inc=1, device_id=place(1, z, c), device_id_type=pl.DeviceIdType.MESH
        )

    @pl.when(sec == 1)
    def _():
        for k in range(1, count):
            forward(1, k).start()

    qkv_in[:, z] = qkv_out[z]
    for k in range(1, count):
        zz = lax.rem(z + k, 4)
        landed(qkv_in.at[:, zz], q_r.at[zz])
    fresh = qkv_in[:, :, :, :128].reshape(256, 128)
    query = qkv_in[:, :, :, 128:].reshape(256, 128)[:, :HD]
    cache_out[...] = fresh
    old = stale[...]
    contract = (((1,), (1,)), ((), ()))
    fresh_scores = lax.dot_general(query, fresh[:, :HD], contract, preferred_element_type=jnp.float32)
    old_scores = lax.dot_general(query, old[:, :HD], contract, preferred_element_type=jnp.float32)
    query_patch = lax.broadcasted_iota(jnp.int32, (256, 256), 0) // 64
    key_patch = lax.broadcasted_iota(jnp.int32, (256, 256), 1) // 64
    is_fresh = key_patch <= query_patch
    scores = jnp.where(is_fresh, fresh_scores, old_scores) * (HD ** -0.5) + bias[0:1, :]
    weights = jnp.exp(scores - jnp.max(scores, axis=1, keepdims=True))
    total = jnp.sum(weights, axis=1, keepdims=True)
    combined = jnp.dot(
        jnp.where(is_fresh, weights, 0.0).astype(jnp.bfloat16), fresh,
        preferred_element_type=jnp.float32,
    ) + jnp.dot(
        jnp.where(is_fresh, 0.0, weights).astype(jnp.bfloat16), old,
        preferred_element_type=jnp.float32,
    )
    att_out[...] = (combined / total).astype(jnp.bfloat16).reshape(4, 4, 16, 128)

    def att_copy(zz):
        return remote(
            att_out.at[:, zz], att_in.at[sec, c], a_s.at[zz], a_r.at[sec, c], place(1, zz, z)
        )

    def own_copy(zz):
        return pltpu.make_async_copy(att_out.at[:, zz], att_in.at[1, c], a_r.at[1, c])

    for zz in range(count):
        stays = jnp.logical_and(sec == 1, jnp.logical_and(z == zz, c == z))

        @pl.when(stays)
        def _():
            own_copy(zz).start()

        @pl.when(jnp.logical_not(stays))
        def _():
            att_copy(zz).start()

    def pred_copy(k):
        return remote(
            pred, pred_in.at[c % 2], p_s.at[k], p_r.at[c % 2],
            place(c // 2, z, lax.rem(c + k, 4)),
        )

    @pl.when(sec == 1)
    def _():
        forwards_landed(1)
        out_projection(1, x_buf, mod)

        def last_rows(p, carry):
            rows = pl.ds(pl.multiple_of(p * 16, 16), 16)
            normed = norm16(x_buf[rows, :])
            fin[rows, :] = (normed * (1.0 + omod[1:2, :]) + omod[0:1, :]).astype(jnp.bfloat16)
            return carry

        lax.fori_loop(0, 4, last_rows, 0)
        pred[...] = jnp.dot(fin[...], proj[...], preferred_element_type=jnp.float32)

        @pl.when(c // 2 == 0)
        def _():
            pred_copy(0).start()

        @pl.when(c // 2 == 1)
        def _():
            pltpu.make_async_copy(pred, pred_in.at[c % 2], p_r.at[c % 2]).start()

        for k in range(1, count):
            pred_copy(k).start()

    for half in range(2):
        landed(pred_in.at[half], p_r.at[half])
    first = pred_in[0]
    guided = first + coef[0, 2] * (pred_in[1] - first)
    lat_out[...] = coef[0, 0] * lat[...] + coef[0, 1] * guided

    @pl.when(sec == 0)
    def _():
        mod_copy.wait_send()
        for k in range(count):
            shard_copy(0, k).wait_send()

    @pl.when(sec == 1)
    def _():
        for k in range(1, count):
            shard_copy(1, k).wait_send()
            forward(0, k).wait_send()
            forward(1, k).wait_send()
            pred_copy(k).wait_send()

        @pl.when(c // 2 == 0)
        def _():
            pred_copy(0).wait_send()

    for k in range(1, count):
        gather(k).wait_send()
        qkv_copy(lax.rem(z + k, 4)).wait_send()
    for zz in range(count):
        stays = jnp.logical_and(sec == 1, jnp.logical_and(z == zz, c == z))

        @pl.when(jnp.logical_not(stays))
        def _():
            att_copy(zz).wait_send()


def fused(
    hidden_states, latent, stale_cache, qkv_weight, out_weight, modulation, out_modulation,
    proj_weight, solver_coef, video_len, text_len, positions,
):
    z = lax.axis_index("seq")
    width = hidden_states.shape[3]
    qkv = qkv_weight[0]
    wqkv = jnp.concatenate(
        [qkv[:, 1], qkv[:, 2], qkv[:, 0], jnp.zeros_like(qkv[:, 0])], axis=1
    )
    wout = out_weight[0].T
    rows = jnp.arange(64)
    row_place = (rows // 16) * 64 + z * 16 + rows % 16
    places = positions.reshape(3, 2, 64).astype(jnp.float32)
    angles = rope_angles(places, HD)
    angles = jnp.where((row_place < TEXT)[None, :, None], 0.0, angles)
    cos, sin = jnp.cos(angles), jnp.sin(angles)
    rest = jnp.zeros((2, 64, HD), jnp.float32)
    cos_t = jnp.concatenate([cos, cos, rest + 1.0], axis=-1)
    sin_t = jnp.concatenate([-sin, sin, rest], axis=-1)
    row_ids = jnp.arange(256)
    text_limit = lax.dynamic_index_in_dim(text_len, z, keepdims=False)
    video_limit = lax.dynamic_index_in_dim(video_len, z // 2, keepdims=False)
    live = jnp.where(row_ids < TEXT, row_ids < text_limit, row_ids - TEXT < video_limit)
    bias = jnp.where(live, 0.0, -jnp.inf).astype(jnp.float32)[None]
    vmem = pl.BlockSpec(memory_space=pltpu.VMEM)
    smem = pl.BlockSpec(memory_space=pltpu.SMEM)
    dma = pltpu.SemaphoreType.DMA
    bf16, f32 = jnp.bfloat16, jnp.float32
    new_latent, new_cache = pl.pallas_call(
        fused_kernel,
        out_shape=(
            jax.ShapeDtypeStruct((64, 64), f32),
            jax.ShapeDtypeStruct((256, 128), bf16),
        ),
        in_specs=[vmem] * 8 + [smem] + [vmem] * 3,
        out_specs=(vmem, vmem),
        scratch_shapes=[
            pltpu.VMEM((64, width), bf16),
            pltpu.VMEM((4, 64, width), bf16),
            pltpu.VMEM((4, 4, 16, 256), bf16),
            pltpu.VMEM((4, 4, 16, 256), bf16),
            pltpu.VMEM((4, 4, 16, 128), bf16),
            pltpu.VMEM((2, 4, 4, 16, 128), bf16),
            pltpu.VMEM((2, 4, HD, width), bf16),
            pltpu.VMEM((6, width), f32),
            pltpu.VMEM((64, width), bf16),
            pltpu.VMEM((64, 64), f32),
            pltpu.VMEM((2, 64, 64), f32),
            dma((3,)), dma((3,)), dma((4,)), dma((4,)), dma((4,)), dma((2, 4)),
            dma((4,)), dma((2, 4)), dma((2, 3)), dma((2, 3)), dma, dma, dma((4,)), dma((2,)),
            pltpu.SemaphoreType.REGULAR,
        ],
        compiler_params=pltpu.CompilerParams(
            collective_id=0, has_side_effects=True, vmem_limit_bytes=40 * 1024 * 1024
        ),
    )(
        hidden_states.reshape(64, width), latent.reshape(64, 64), stale_cache[0, 0, 0], wqkv, wout,
        modulation[0], out_modulation, proj_weight, solver_coef, cos_t, sin_t, bias,
    )
    return new_latent.reshape(latent.shape), new_cache.reshape(stale_cache.shape)


def per_device(*args):
    hidden_states, latent, stale_cache, qkv_weight = args[:4]
    sizes = tuple(lax.axis_size(axis) for axis in ("section", "seq", "cfg"))
    small = (
        sizes == (2, 4, 4)
        and hidden_states.shape[:3] == (1, 4, 16)
        and latent.shape == (1, 4, 16, 64)
        and stale_cache.shape == (1, 1, 1, 256, 128)
        and qkv_weight.shape[3] == HD
    )
    return fused(*args) if small else general(*args)


def solution(mesh):
    return jax.shard_map(
        per_device,
        mesh=mesh,
        in_specs=(
            P("cfg", None, "seq", None),
            P("section", None, "seq", None),
            P("section", "cfg", "seq", None, None),
            P("section", None, None, "cfg"),
            P("section", "seq", "cfg"),
            P("section", None, None),
            P(),
            P(),
            P("section", None),
            P(),
            P(),
            P(None, None, None, "seq"),
        ),
        out_specs=(P("section", None, "seq", None), P("section", "cfg", "seq", None, None)),
        check_vma=False,
    )
```

```python
import math

import jax
import jax.numpy as jnp
from jax import lax
from jax.experimental import pallas as pl
from jax.experimental.pallas import tpu as pltpu
from jax.sharding import PartitionSpec as P

HD = 64
TEXT = 226


def from_behind(value, axis, steps):
    count = lax.axis_size(axis)
    pairs = [(source, (source + steps) % count) for source in range(count)]
    return lax.ppermute(value, axis, pairs)


def row_norm(values):
    centered = values - jnp.mean(values, axis=-1, keepdims=True)
    return centered * lax.rsqrt(jnp.mean(centered * centered, axis=-1, keepdims=True) + 1e-05)


def head_norm(values):
    centered = values - jnp.mean(values, axis=-1, keepdims=True)
    return centered * lax.rsqrt(jnp.mean(centered * centered, axis=-1, keepdims=True) + 1e-06)


def rope_angles(places, head_size):
    half_size = head_size // 2
    pairs_t = head_size // 8
    pairs_h = (half_size - pairs_t) // 2
    pair_index = jnp.arange(half_size)
    first_part = pair_index < pairs_t
    second_part = jnp.logical_and(pair_index >= pairs_t, pair_index < pairs_t + pairs_h)
    third_part = pair_index >= pairs_t + pairs_h
    local_index = jnp.where(
        first_part,
        pair_index,
        jnp.where(second_part, pair_index - pairs_t, pair_index - pairs_t - pairs_h),
    )
    axis_span = jnp.where(first_part, 2 * pairs_t, 2 * pairs_h)
    frequency = jnp.exp(
        -math.log(10000.0) * 2.0 * local_index.astype(jnp.float32) / axis_span.astype(jnp.float32)
    )
    angles = places[0][..., None] * first_part.astype(jnp.float32)
    angles = angles + places[1][..., None] * second_part.astype(jnp.float32)
    angles = angles + places[2][..., None] * third_part.astype(jnp.float32)
    return angles * frequency


def rotate(values, cos_table, sin_table):
    half_size = values.shape[-1] // 2
    first_half = values[..., :half_size]
    second_half = values[..., half_size:]
    return jnp.concatenate(
        [
            first_half * cos_table - second_half * sin_table,
            second_half * cos_table + first_half * sin_table,
        ],
        axis=-1,
    )


def spread(values):
    return lax.all_gather(values, "cfg", axis=0, tiled=True)


def handoff(values):
    return from_behind(values, "section", 1)


def general(
    hidden_states,
    latent,
    stale_cache,
    qkv_weight,
    out_weight,
    modulation,
    out_modulation,
    proj_weight,
    solver_coef,
    video_len,
    text_len,
    positions,
):
    section_id = lax.axis_index("section")
    shard_id = lax.axis_index("seq")
    seq_devices = lax.axis_size("seq")
    patches = hidden_states.shape[1]
    patch_dev = hidden_states.shape[2]
    width = hidden_states.shape[3]
    patch_len = patch_dev * seq_devices
    total_len = patch_len * patches
    group_heads = qkv_weight.shape[3] // HD
    qkv_full = qkv_weight[0].reshape(width, 3, group_heads, HD)
    out_full = lax.all_gather(out_weight[0], "seq", axis=0, tiled=True).reshape(
        width, group_heads, HD
    )
    mod_rows = modulation[0]
    stale_rows = stale_cache[0, 0, 0]
    my_sequence = shard_id // group_heads
    row_ids = jnp.arange(total_len)
    text_limit = lax.dynamic_index_in_dim(text_len, my_sequence, keepdims=False)
    video_limit = lax.dynamic_index_in_dim(video_len, my_sequence // 2, keepdims=False)
    live_keys = jnp.where(row_ids < TEXT, row_ids < text_limit, row_ids - TEXT < video_limit)
    key_patch = row_ids // patch_len
    query_block = patch_len
    while query_block > 1024 and query_block % 2 == 0:
        query_block = query_block // 2
    scale_factor = HD ** (-0.5)
    key_cache = stale_rows
    received = hidden_states
    first_patch = 0
    for tick_id in range(2):
        hidden = jnp.where(section_id == 0, hidden_states, received)
        run_key_cache = stale_rows
        patch_count = hidden.shape[1]
        row_place = (
            (first_patch + jnp.arange(patch_count))[:, None] * patch_len
            + shard_id * patch_dev
            + jnp.arange(patch_dev)[None, :]
        )
        text_rows = (row_place < TEXT)[:, :, None]
        run_normed = row_norm(hidden.astype(jnp.float32))
        shift_rows = jnp.where(text_rows, mod_rows[3], mod_rows[0])
        scale_rows = jnp.where(text_rows, mod_rows[4], mod_rows[1])
        gate_rows = jnp.where(text_rows, mod_rows[5], mod_rows[2])
        mixed_rows = (run_normed * (1.0 + scale_rows) + shift_rows).astype(jnp.bfloat16)
        mixed_rows = spread(mixed_rows)
        seq_count = mixed_rows.shape[0]
        projected = jnp.einsum(
            "spqd,djge->sgjpqe", mixed_rows, qkv_full, preferred_element_type=jnp.float32
        )
        places = lax.dynamic_slice_in_dim(positions, first_patch, patch_count, 2).astype(
            jnp.float32
        )
        angles = rope_angles(places, HD)
        angles = jnp.where(text_rows[None], 0.0, angles)
        angles = jnp.repeat(angles, 2, axis=0)[:, None]
        cos_table = jnp.cos(angles)
        sin_table = jnp.sin(angles)
        queries = rotate(head_norm(projected[:, :, 0]), cos_table, sin_table)
        key_part = rotate(head_norm(projected[:, :, 1]), cos_table, sin_table)
        stacked = jnp.stack([queries, key_part, projected[:, :, 2]], axis=2).astype(jnp.bfloat16)
        outgoing = stacked.reshape(seq_count * group_heads, 3, patch_count, patch_dev * HD)
        incoming = lax.all_to_all(outgoing, "seq", split_axis=0, concat_axis=3, tiled=True)
        incoming = incoming.reshape(3, patch_count * patch_len, HD)
        fresh_rows = jnp.concatenate([incoming[1], incoming[2]], axis=-1)
        run_key_cache = lax.dynamic_update_slice_in_dim(
            run_key_cache, fresh_rows, first_patch * patch_len, 0
        )
        block_count = patch_count * patch_len // query_block

        def attend(work_item):
            query_rows, block_id = work_item
            patch_now = first_patch + block_id * query_block // patch_len
            key_rows = jnp.where((key_patch <= patch_now)[:, None], run_key_cache, stale_rows)
            scores = (
                jnp.dot(query_rows, key_rows[:, :HD].T, preferred_element_type=jnp.float32)
                * scale_factor
            )
            scores = jnp.where(live_keys[None, :], scores, -jnp.inf)
            row_max = jnp.max(scores, axis=1, keepdims=True)
            weights = jnp.exp(scores - row_max)
            row_sum = jnp.sum(weights, axis=1, keepdims=True)
            combined = jnp.dot(
                weights.astype(jnp.bfloat16), key_rows[:, HD:], preferred_element_type=jnp.float32
            )
            return (combined / row_sum).astype(jnp.bfloat16)

        attended = lax.map(
            attend, (incoming[0].reshape(block_count, query_block, HD), jnp.arange(block_count))
        )
        attended = attended.reshape(patch_count, seq_devices, patch_dev * HD)[None]
        returned = lax.all_to_all(attended, "seq", split_axis=2, concat_axis=0, tiled=True)
        returned = returned.reshape(seq_count, group_heads, patch_count, patch_dev, HD)
        update = lax.psum_scatter(
            jnp.einsum("sgpqe,dge->spqd", returned, out_full, preferred_element_type=jnp.float32),
            "cfg",
            scatter_dimension=0,
            tiled=True,
        )
        result = (hidden.astype(jnp.float32) + gate_rows * update).astype(jnp.bfloat16)
        key_cache = jnp.where(section_id == tick_id, run_key_cache, key_cache)
        if tick_id == 0:
            received = handoff(result)
    normed = row_norm(result.astype(jnp.float32))
    normed_out = (normed * (1.0 + out_modulation[1]) + out_modulation[0]).astype(jnp.bfloat16)
    own_values = jnp.einsum(
        "spqd,do->spqo", normed_out, proj_weight, preferred_element_type=jnp.float32
    )
    all_values = lax.all_gather(own_values, ("section", "cfg"), axis=0, tiled=True)
    last = all_values.shape[0] // 2
    predicted = lax.dynamic_slice_in_dim(all_values, last + 2 * section_id, 2, 0)
    solver_row = solver_coef[0]
    guided = predicted[0] + solver_row[2] * (predicted[1] - predicted[0])
    new_latent = (solver_row[0] * latent[0] + solver_row[1] * guided)[None]
    return (new_latent, key_cache[None, None, None])


def fused_kernel(
    hid, lat, stale, wqkv, wout, mod, omod, proj, coef, texts, videos, cos_t, sin_t,
    lat_out, cache_out,
    x_buf, mix, qkv_out, qkv_in, att_out, att_in, wo, mod0, fin, pred, pred_in,
    g_s, g_r, q_s, q_r, a_s, a_r, w_s, w_r, f_s, f_r, m_s, m_r, p_s, p_r, go,
):
    sec = lax.axis_index("section")
    z = lax.axis_index("seq")
    c = lax.axis_index("cfg")
    width = hid.shape[1]
    shard = wout.shape[1]
    count = 4

    def place(section, seq, cfg):
        return {"section": section, "seq": seq, "cfg": cfg}

    def remote(src, dst, send, recv, target):
        return pltpu.make_async_remote_copy(
            src_ref=src, dst_ref=dst, send_sem=send, recv_sem=recv,
            device_id=target, device_id_type=pl.DeviceIdType.MESH,
        )

    def landed(dst, sem):
        pltpu.make_async_copy(dst, dst, sem).wait()

    barrier = pltpu.get_barrier_semaphore()
    everyone = 2 * count * count
    me = (sec * count + z) * count + c

    def greet(i, carry):
        other = lax.rem(me + i, everyone)
        pl.semaphore_signal(
            barrier, inc=1,
            device_id=place(other // 16, lax.rem(other // 4, 4), lax.rem(other, 4)),
            device_id_type=pl.DeviceIdType.MESH,
        )
        return carry

    lax.fori_loop(1, everyone, greet, 0)
    pl.semaphore_wait(barrier, everyone - 1)

    own_cols = pl.ds(pl.multiple_of(z * shard, 128), shard)

    def shard_copy(layer, k):
        return remote(
            wout, wo.at[layer, c, :, own_cols], w_s.at[k], w_r.at[layer, z],
            place(1, lax.rem(z + k, 4), c),
        )

    over_x = c + 1 - 2 * (c % 2)
    over_y = lax.rem(c + 2, 4)
    across = lax.rem(over_x + 2, 4)
    steps = (
        (c, 0, over_x), (c, 1, over_x), (c, 1, over_y), (c, 0, over_y),
        (over_x, 0, over_y), (over_y, 1, over_x),
    )
    arrivals = ((over_x, 0), (over_x, 1), (over_y, 1), (over_y, 0), (across, 0), (across, 1))

    def relay(blocks, sends, receives, j, section):
        owner, half, target = steps[j]
        part = blocks.at[owner, half * 32 : half * 32 + 32]
        return remote(part, part, sends.at[j], receives.at[j], place(section, z, target))

    def relay_landed(blocks, receives, j):
        owner, half = arrivals[j]
        landed(blocks.at[owner, half * 32 : half * 32 + 32], receives.at[j])

    def forward(layer, j):
        return relay(wo.at[layer], f_s.at[layer], f_r.at[layer], j, 1)

    def forward_landed(layer, j):
        relay_landed(wo.at[layer], f_r.at[layer], j)

    def pass_on(layer):
        forward_landed(layer, 0)
        forward(layer, 4).start()
        forward_landed(layer, 2)
        forward(layer, 5).start()

    def shards_landed(layer):
        for zz in range(count):
            dst = wo.at[layer, c, :, zz * shard : (zz + 1) * shard]
            if layer == 0:
                landed(dst, w_r.at[layer, zz])
            else:
                @pl.when(z != zz)
                def _():
                    landed(dst, w_r.at[layer, zz])

    def forwards_landed(layer):
        for j in (1, 3, 4, 5):
            forward_landed(layer, j)

    def text_mask(start, rows):
        i = lax.broadcasted_iota(jnp.int32, (rows, 1), 0) + start
        return (i // 16) * 64 + z * 16 + i % 16 < TEXT

    def norm16(values):
        values = values.astype(jnp.float32)
        centered = values - jnp.mean(values, axis=-1, keepdims=True)
        return centered * lax.rsqrt(jnp.mean(centered * centered, axis=-1, keepdims=True) + 1e-05)

    def out_projection(layer, prev, gates):
        for h in range(count):
            landed(att_in.at[layer, h], a_r.at[layer, h])
        rows = [att_in[layer, h].reshape(64, 128)[:, HD:] for h in range(count)]
        joined = jnp.concatenate(rows, axis=1)
        text = text_mask(0, 64)
        for part in range(4):
            cols = slice(part * (width // 4), (part + 1) * (width // 4))
            weight = wo[layer, :, :, cols].reshape(4 * HD, width // 4)
            update = jnp.dot(joined, weight, preferred_element_type=jnp.float32)
            gate = jnp.where(text, gates[5:6, cols], gates[2:3, cols])
            x_buf[:, cols] = (prev[:, cols].astype(jnp.float32) + gate * update).astype(jnp.bfloat16)

    mod_copy = remote(mod, mod0, m_s, m_r, place(1, z, c))

    @pl.when(sec == 0)
    def _():
        mod_copy.start()
        for k in range(count):
            shard_copy(0, k).start()
        x_buf[...] = hid[...]

    @pl.when(sec == 1)
    def _():
        for k in range(1, count):
            shard_copy(1, k).start()
        wo[1, c, :, own_cols] = wout[...]
        shards_landed(0)
        pl.semaphore_wait(go, 1)
        for j in (0, 2, 1, 3):
            forward(0, j).start()
        pass_on(0)
        shards_landed(1)
        mod_copy.wait_recv()
        forwards_landed(0)
        out_projection(0, hid, mod0)

    def mix_rows(p, carry):
        rows = pl.ds(pl.multiple_of(p * 16, 16), 16)
        text = text_mask(p * 16, 16)
        normed = norm16(x_buf[rows, :])
        scale = jnp.where(text, mod[4:5, :], mod[1:2, :])
        shift = jnp.where(text, mod[3:4, :], mod[0:1, :])
        mix[c, rows, :] = (normed * (1.0 + scale) + shift).astype(jnp.bfloat16)
        return carry

    def gather(j):
        return relay(mix, g_s, g_r, j, sec)

    lax.fori_loop(0, 2, mix_rows, 0)
    gather(0).start()
    lax.fori_loop(2, 4, mix_rows, 0)
    for j in (2, 1, 3):
        gather(j).start()

    contract = (((1,), (1,)), ((), ()))
    lane = lax.broadcasted_iota(jnp.int32, (1, 128), 1)
    head = lane < HD
    low = (lane // 32) % 2 == 0

    def prepare(values, cos_table, sin_table):
        mean = jnp.sum(jnp.where(head, values, 0.0), axis=-1, keepdims=True) * (1.0 / HD)
        centered = values - mean
        square = jnp.where(head, centered * centered, 0.0)
        scale = lax.rsqrt(jnp.sum(square, axis=-1, keepdims=True) * (1.0 / HD) + 1e-06)
        normed = jnp.where(head, centered * scale, values)
        swapped = jnp.where(low, pltpu.roll(normed, 96, 1), pltpu.roll(normed, 32, 1))
        return (normed * cos_table + swapped * sin_table).astype(jnp.bfloat16).reshape(4, 16, 128)

    def qkv_copy(s):
        return remote(
            qkv_out.at[s], qkv_in.at[:, z], q_s.at[s], q_r.at[z], place(sec, s, c)
        )

    for k, s in enumerate((c, over_x, over_y, across)):
        if k == 1:
            relay_landed(mix, g_r, 0)
            gather(4).start()
            relay_landed(mix, g_r, 2)
            gather(5).start()
            relay_landed(mix, g_r, 1)
        if k == 2:
            relay_landed(mix, g_r, 3)
        if k == 3:
            relay_landed(mix, g_r, 4)
            relay_landed(mix, g_r, 5)
        projected = lax.dot_general(mix[s], wqkv[...], contract, preferred_element_type=jnp.float32)
        cos_table = cos_t[s // 2]
        sin_table = sin_t[s // 2]
        kv = prepare(projected[:, HD:], cos_table, sin_table)
        qq = prepare(projected[:, :128], cos_table, sin_table)

        qkv_out[s, :, :, :128] = kv
        qkv_out[s, :, :, 128:] = qq

        @pl.when(s != z)
        def _():
            qkv_copy(s).start()

    @pl.when(sec == 0)
    def _():
        pl.semaphore_signal(
            go, inc=1, device_id=place(1, z, c), device_id_type=pl.DeviceIdType.MESH
        )

    @pl.when(sec == 1)
    def _():
        for j in (0, 2, 1, 3):
            forward(1, j).start()

    qkv_in[:, z] = qkv_out[z]
    for k in range(1, count):
        zz = lax.rem(z + k, 4)
        landed(qkv_in.at[:, zz], q_r.at[zz])

    @pl.when(sec == 1)
    def _():
        pass_on(1)

    fresh = qkv_in[:, :, :, :128].reshape(256, 128)
    query = qkv_in[:, :, :, 128:].reshape(256, 128)[:, :HD]
    cache_out[...] = fresh
    old = stale[...]
    key_row = lax.broadcasted_iota(jnp.int32, (1, 256), 1)
    limit = jnp.where(key_row < TEXT, texts[z], TEXT + videos[z // 2])
    bias = jnp.where(key_row < limit, 0.0, -jnp.inf)
    fresh_scores = lax.dot_general(query, fresh[:, :HD], contract, preferred_element_type=jnp.float32)
    old_scores = lax.dot_general(query, old[:, :HD], contract, preferred_element_type=jnp.float32)
    query_patch = lax.broadcasted_iota(jnp.int32, (256, 256), 0) // 64
    key_patch = lax.broadcasted_iota(jnp.int32, (256, 256), 1) // 64
    is_fresh = key_patch <= query_patch
    scores = jnp.where(is_fresh, fresh_scores, old_scores) * (HD ** -0.5) + bias
    weights = jnp.exp(scores - jnp.max(scores, axis=1, keepdims=True))
    total = jnp.sum(weights, axis=1, keepdims=True)
    combined = jnp.dot(
        jnp.where(is_fresh, weights, 0.0).astype(jnp.bfloat16), fresh,
        preferred_element_type=jnp.float32,
    ) + jnp.dot(
        jnp.where(is_fresh, 0.0, weights).astype(jnp.bfloat16), old,
        preferred_element_type=jnp.float32,
    )
    att_out[...] = (combined / total).astype(jnp.bfloat16).reshape(4, 4, 16, 128)

    def att_copy(zz):
        return remote(
            att_out.at[:, zz], att_in.at[sec, c], a_s.at[zz], a_r.at[sec, c], place(1, zz, z)
        )

    def own_copy(zz):
        return pltpu.make_async_copy(att_out.at[:, zz], att_in.at[1, c], a_r.at[1, c])

    for zz in range(count):
        stays = jnp.logical_and(sec == 1, jnp.logical_and(z == zz, c == z))

        @pl.when(stays)
        def _():
            own_copy(zz).start()

        @pl.when(jnp.logical_not(stays))
        def _():
            att_copy(zz).start()

    def pred_copy(k):
        return remote(
            pred, pred_in.at[c % 2], p_s.at[k], p_r.at[c % 2],
            place(c // 2, z, lax.rem(c + k, 4)),
        )

    @pl.when(sec == 1)
    def _():
        forwards_landed(1)
        out_projection(1, x_buf, mod)

        def last_rows(p, carry):
            rows = pl.ds(pl.multiple_of(p * 16, 16), 16)
            normed = norm16(x_buf[rows, :])
            fin[rows, :] = (normed * (1.0 + omod[1:2, :]) + omod[0:1, :]).astype(jnp.bfloat16)
            return carry

        lax.fori_loop(0, 4, last_rows, 0)
        pred[...] = lax.dot_general(
            fin[...], proj[...], contract, preferred_element_type=jnp.float32
        )

        @pl.when(c // 2 == 0)
        def _():
            pred_copy(0).start()

        @pl.when(c // 2 == 1)
        def _():
            pltpu.make_async_copy(pred, pred_in.at[c % 2], p_r.at[c % 2]).start()

        for k in range(1, count):
            pred_copy(k).start()

    for half in range(2):
        landed(pred_in.at[half], p_r.at[half])
    first = pred_in[0]
    guided = first + coef[0, 2] * (pred_in[1] - first)
    lat_out[...] = coef[0, 0] * lat[...] + coef[0, 1] * guided

    @pl.when(sec == 0)
    def _():
        mod_copy.wait_send()
        for k in range(count):
            shard_copy(0, k).wait_send()

    @pl.when(sec == 1)
    def _():
        for k in range(1, count):
            shard_copy(1, k).wait_send()
            pred_copy(k).wait_send()
        for j in range(6):
            forward(0, j).wait_send()
            forward(1, j).wait_send()

        @pl.when(c // 2 == 0)
        def _():
            pred_copy(0).wait_send()

    for j in range(6):
        gather(j).wait_send()
    for k in range(1, count):
        qkv_copy(lax.rem(z + k, 4)).wait_send()
    for zz in range(count):
        stays = jnp.logical_and(sec == 1, jnp.logical_and(z == zz, c == z))

        @pl.when(jnp.logical_not(stays))
        def _():
            att_copy(zz).wait_send()


def fused(
    hidden_states, latent, stale_cache, qkv_weight, out_weight, modulation, out_modulation,
    proj_weight, solver_coef, video_len, text_len, positions,
):
    z = lax.axis_index("seq")
    width = hidden_states.shape[3]
    wqkv = qkv_weight[0].transpose(1, 2, 0).reshape(3 * HD, width)
    wout = out_weight[0].T
    rows = jnp.arange(64)
    row_place = (rows // 16) * 64 + z * 16 + rows % 16
    places = positions.reshape(3, 2, 64).astype(jnp.float32)
    angles = rope_angles(places, HD)
    angles = jnp.where((row_place < TEXT)[None, :, None], 0.0, angles)
    cos, sin = jnp.cos(angles), jnp.sin(angles)
    rest = jnp.zeros((2, 64, HD), jnp.float32)
    cos_t = jnp.concatenate([cos, cos, rest + 1.0], axis=-1)
    sin_t = jnp.concatenate([-sin, sin, rest], axis=-1)
    vmem = pl.BlockSpec(memory_space=pltpu.VMEM)
    smem = pl.BlockSpec(memory_space=pltpu.SMEM)
    dma = pltpu.SemaphoreType.DMA
    bf16, f32 = jnp.bfloat16, jnp.float32
    new_latent, new_cache = pl.pallas_call(
        fused_kernel,
        out_shape=(
            jax.ShapeDtypeStruct((64, 64), f32),
            jax.ShapeDtypeStruct((256, 128), bf16),
        ),
        in_specs=[vmem] * 8 + [smem] * 3 + [vmem] * 2,
        out_specs=(vmem, vmem),
        scratch_shapes=[
            pltpu.VMEM((64, width), bf16),
            pltpu.VMEM((4, 64, width), bf16),
            pltpu.VMEM((4, 4, 16, 256), bf16),
            pltpu.VMEM((4, 4, 16, 256), bf16),
            pltpu.VMEM((4, 4, 16, 128), bf16),
            pltpu.VMEM((2, 4, 4, 16, 128), bf16),
            pltpu.VMEM((2, 4, HD, width), bf16),
            pltpu.VMEM((6, width), f32),
            pltpu.VMEM((64, width), bf16),
            pltpu.VMEM((64, 64), f32),
            pltpu.VMEM((2, 64, 64), f32),
            dma((6,)), dma((6,)), dma((4,)), dma((4,)), dma((4,)), dma((2, 4)),
            dma((4,)), dma((2, 4)), dma((2, 6)), dma((2, 6)), dma, dma, dma((4,)), dma((2,)),
            pltpu.SemaphoreType.REGULAR,
        ],
        compiler_params=pltpu.CompilerParams(
            collective_id=0, has_side_effects=True, vmem_limit_bytes=40 * 1024 * 1024
        ),
    )(
        hidden_states.reshape(64, width), latent.reshape(64, 64), stale_cache[0, 0, 0], wqkv, wout,
        modulation[0], out_modulation, proj_weight.T, solver_coef, text_len, video_len,
        cos_t, sin_t,
    )
    return new_latent.reshape(latent.shape), new_cache.reshape(stale_cache.shape)


def per_device(*args):
    hidden_states, latent, stale_cache, qkv_weight = args[:4]
    sizes = tuple(lax.axis_size(axis) for axis in ("section", "seq", "cfg"))
    small = (
        sizes == (2, 4, 4)
        and hidden_states.shape[:3] == (1, 4, 16)
        and latent.shape == (1, 4, 16, 64)
        and stale_cache.shape == (1, 1, 1, 256, 128)
        and qkv_weight.shape[3] == HD
    )
    return fused(*args) if small else general(*args)


def solution(mesh):
    return jax.shard_map(
        per_device,
        mesh=mesh,
        in_specs=(
            P("cfg", None, "seq", None),
            P("section", None, "seq", None),
            P("section", "cfg", "seq", None, None),
            P("section", None, None, "cfg"),
            P("section", "seq", "cfg"),
            P("section", None, None),
            P(),
            P(),
            P("section", None),
            P(),
            P(),
            P(None, None, None, "seq"),
        ),
        out_specs=(P("section", None, "seq", None), P("section", "cfg", "seq", None, None)),
        check_vma=False,
    )
```

```python
import math

import jax
import jax.numpy as jnp
from jax import lax
from jax.experimental import pallas as pl
from jax.experimental.pallas import tpu as pltpu
from jax.sharding import PartitionSpec as P

HD = 64
TEXT = 226


def from_behind(value, axis, steps):
    count = lax.axis_size(axis)
    pairs = [(source, (source + steps) % count) for source in range(count)]
    return lax.ppermute(value, axis, pairs)


def row_norm(values):
    centered = values - jnp.mean(values, axis=-1, keepdims=True)
    return centered * lax.rsqrt(jnp.mean(centered * centered, axis=-1, keepdims=True) + 1e-05)


def head_norm(values):
    centered = values - jnp.mean(values, axis=-1, keepdims=True)
    return centered * lax.rsqrt(jnp.mean(centered * centered, axis=-1, keepdims=True) + 1e-06)


def rope_angles(places, head_size):
    half_size = head_size // 2
    pairs_t = head_size // 8
    pairs_h = (half_size - pairs_t) // 2
    pair_index = jnp.arange(half_size)
    first_part = pair_index < pairs_t
    second_part = jnp.logical_and(pair_index >= pairs_t, pair_index < pairs_t + pairs_h)
    third_part = pair_index >= pairs_t + pairs_h
    local_index = jnp.where(
        first_part,
        pair_index,
        jnp.where(second_part, pair_index - pairs_t, pair_index - pairs_t - pairs_h),
    )
    axis_span = jnp.where(first_part, 2 * pairs_t, 2 * pairs_h)
    frequency = jnp.exp(
        -math.log(10000.0) * 2.0 * local_index.astype(jnp.float32) / axis_span.astype(jnp.float32)
    )
    angles = places[0][..., None] * first_part.astype(jnp.float32)
    angles = angles + places[1][..., None] * second_part.astype(jnp.float32)
    angles = angles + places[2][..., None] * third_part.astype(jnp.float32)
    return angles * frequency


def rotate(values, cos_table, sin_table):
    half_size = values.shape[-1] // 2
    first_half = values[..., :half_size]
    second_half = values[..., half_size:]
    return jnp.concatenate(
        [
            first_half * cos_table - second_half * sin_table,
            second_half * cos_table + first_half * sin_table,
        ],
        axis=-1,
    )


def spread(values):
    return lax.all_gather(values, "cfg", axis=0, tiled=True)


def handoff(values):
    return from_behind(values, "section", 1)


def general(
    hidden_states,
    latent,
    stale_cache,
    qkv_weight,
    out_weight,
    modulation,
    out_modulation,
    proj_weight,
    solver_coef,
    video_len,
    text_len,
    positions,
):
    section_id = lax.axis_index("section")
    shard_id = lax.axis_index("seq")
    seq_devices = lax.axis_size("seq")
    patches = hidden_states.shape[1]
    patch_dev = hidden_states.shape[2]
    width = hidden_states.shape[3]
    patch_len = patch_dev * seq_devices
    total_len = patch_len * patches
    group_heads = qkv_weight.shape[3] // HD
    qkv_full = qkv_weight[0].reshape(width, 3, group_heads, HD)
    out_full = lax.all_gather(out_weight[0], "seq", axis=0, tiled=True).reshape(
        width, group_heads, HD
    )
    mod_rows = modulation[0]
    stale_rows = stale_cache[0, 0, 0]
    my_sequence = shard_id // group_heads
    row_ids = jnp.arange(total_len)
    text_limit = lax.dynamic_index_in_dim(text_len, my_sequence, keepdims=False)
    video_limit = lax.dynamic_index_in_dim(video_len, my_sequence // 2, keepdims=False)
    live_keys = jnp.where(row_ids < TEXT, row_ids < text_limit, row_ids - TEXT < video_limit)
    key_patch = row_ids // patch_len
    query_block = patch_len
    while query_block > 1024 and query_block % 2 == 0:
        query_block = query_block // 2
    scale_factor = HD ** (-0.5)
    key_cache = stale_rows
    received = hidden_states
    first_patch = 0
    for tick_id in range(2):
        hidden = jnp.where(section_id == 0, hidden_states, received)
        run_key_cache = stale_rows
        patch_count = hidden.shape[1]
        row_place = (
            (first_patch + jnp.arange(patch_count))[:, None] * patch_len
            + shard_id * patch_dev
            + jnp.arange(patch_dev)[None, :]
        )
        text_rows = (row_place < TEXT)[:, :, None]
        run_normed = row_norm(hidden.astype(jnp.float32))
        shift_rows = jnp.where(text_rows, mod_rows[3], mod_rows[0])
        scale_rows = jnp.where(text_rows, mod_rows[4], mod_rows[1])
        gate_rows = jnp.where(text_rows, mod_rows[5], mod_rows[2])
        mixed_rows = (run_normed * (1.0 + scale_rows) + shift_rows).astype(jnp.bfloat16)
        mixed_rows = spread(mixed_rows)
        seq_count = mixed_rows.shape[0]
        projected = jnp.einsum(
            "spqd,djge->sgjpqe", mixed_rows, qkv_full, preferred_element_type=jnp.float32
        )
        places = lax.dynamic_slice_in_dim(positions, first_patch, patch_count, 2).astype(
            jnp.float32
        )
        angles = rope_angles(places, HD)
        angles = jnp.where(text_rows[None], 0.0, angles)
        angles = jnp.repeat(angles, 2, axis=0)[:, None]
        cos_table = jnp.cos(angles)
        sin_table = jnp.sin(angles)
        queries = rotate(head_norm(projected[:, :, 0]), cos_table, sin_table)
        key_part = rotate(head_norm(projected[:, :, 1]), cos_table, sin_table)
        stacked = jnp.stack([queries, key_part, projected[:, :, 2]], axis=2).astype(jnp.bfloat16)
        outgoing = stacked.reshape(seq_count * group_heads, 3, patch_count, patch_dev * HD)
        incoming = lax.all_to_all(outgoing, "seq", split_axis=0, concat_axis=3, tiled=True)
        incoming = incoming.reshape(3, patch_count * patch_len, HD)
        fresh_rows = jnp.concatenate([incoming[1], incoming[2]], axis=-1)
        run_key_cache = lax.dynamic_update_slice_in_dim(
            run_key_cache, fresh_rows, first_patch * patch_len, 0
        )
        block_count = patch_count * patch_len // query_block

        def attend(work_item):
            query_rows, block_id = work_item
            patch_now = first_patch + block_id * query_block // patch_len
            key_rows = jnp.where((key_patch <= patch_now)[:, None], run_key_cache, stale_rows)
            scores = (
                jnp.dot(query_rows, key_rows[:, :HD].T, preferred_element_type=jnp.float32)
                * scale_factor
            )
            scores = jnp.where(live_keys[None, :], scores, -jnp.inf)
            row_max = jnp.max(scores, axis=1, keepdims=True)
            weights = jnp.exp(scores - row_max)
            row_sum = jnp.sum(weights, axis=1, keepdims=True)
            combined = jnp.dot(
                weights.astype(jnp.bfloat16), key_rows[:, HD:], preferred_element_type=jnp.float32
            )
            return (combined / row_sum).astype(jnp.bfloat16)

        attended = lax.map(
            attend, (incoming[0].reshape(block_count, query_block, HD), jnp.arange(block_count))
        )
        attended = attended.reshape(patch_count, seq_devices, patch_dev * HD)[None]
        returned = lax.all_to_all(attended, "seq", split_axis=2, concat_axis=0, tiled=True)
        returned = returned.reshape(seq_count, group_heads, patch_count, patch_dev, HD)
        update = lax.psum_scatter(
            jnp.einsum("sgpqe,dge->spqd", returned, out_full, preferred_element_type=jnp.float32),
            "cfg",
            scatter_dimension=0,
            tiled=True,
        )
        result = (hidden.astype(jnp.float32) + gate_rows * update).astype(jnp.bfloat16)
        key_cache = jnp.where(section_id == tick_id, run_key_cache, key_cache)
        if tick_id == 0:
            received = handoff(result)
    normed = row_norm(result.astype(jnp.float32))
    normed_out = (normed * (1.0 + out_modulation[1]) + out_modulation[0]).astype(jnp.bfloat16)
    own_values = jnp.einsum(
        "spqd,do->spqo", normed_out, proj_weight, preferred_element_type=jnp.float32
    )
    all_values = lax.all_gather(own_values, ("section", "cfg"), axis=0, tiled=True)
    last = all_values.shape[0] // 2
    predicted = lax.dynamic_slice_in_dim(all_values, last + 2 * section_id, 2, 0)
    solver_row = solver_coef[0]
    guided = predicted[0] + solver_row[2] * (predicted[1] - predicted[0])
    new_latent = (solver_row[0] * latent[0] + solver_row[1] * guided)[None]
    return (new_latent, key_cache[None, None, None])


def fused_kernel(
    hid_hbm, lat_hbm, stale_hbm, wqkv_hbm, wout_hbm, mod_hbm, omod_hbm, proj_hbm, coef, texts, videos, cos_t, sin_t,
    lat_out, cache_out,
    x_buf, lat, stale, wqkv, wout, mod, omod, proj, loads,
    mix, qkv_out, qkv_in, att_out, att_in, wo, mod0, fin, pred, pred_in,
    g_s, g_r, q_s, q_r, a_s, a_r, w_s, w_r, f_s, f_r, m_s, m_r, p_s, p_r, go,
):
    sec = lax.axis_index("section")
    z = lax.axis_index("seq")
    c = lax.axis_index("cfg")
    width = hid_hbm.shape[1]
    shard = wout.shape[1]
    count = 4

    def place(section, seq, cfg):
        return {"section": section, "seq": seq, "cfg": cfg}

    def remote(src, dst, send, recv, target):
        return pltpu.make_async_remote_copy(
            src_ref=src, dst_ref=dst, send_sem=send, recv_sem=recv,
            device_id=target, device_id_type=pl.DeviceIdType.MESH,
        )

    def landed(dst, sem):
        pltpu.make_async_copy(dst, dst, sem).wait()

    barrier = pltpu.get_barrier_semaphore()
    everyone = 2 * count * count
    me = (sec * count + z) * count + c

    def greet(i, carry):
        other = lax.rem(me + i, everyone)
        pl.semaphore_signal(
            barrier, inc=1,
            device_id=place(other // 16, lax.rem(other // 4, 4), lax.rem(other, 4)),
            device_id_type=pl.DeviceIdType.MESH,
        )
        return carry

    sources = (hid_hbm, mod_hbm, wout_hbm, wqkv_hbm, stale_hbm, lat_hbm, omod_hbm, proj_hbm)
    targets = (x_buf, mod, wout, wqkv, stale, lat, omod, proj)
    local = [
        pltpu.make_async_copy(source, target, loads.at[i])
        for i, (source, target) in enumerate(zip(sources, targets))
    ]
    for copy in local:
        copy.start()
    lax.fori_loop(1, everyone, greet, 0)

    own_cols = pl.ds(pl.multiple_of(z * shard, 128), shard)

    def shard_copy(layer, k):
        return remote(
            wout, wo.at[layer, c, :, own_cols], w_s.at[k], w_r.at[layer, z],
            place(1, lax.rem(z + k, 4), c),
        )

    over_x = c + 1 - 2 * (c % 2)
    over_y = lax.rem(c + 2, 4)
    across = lax.rem(over_x + 2, 4)
    steps = (
        (c, 0, over_x), (c, 1, over_x), (c, 1, over_y), (c, 0, over_y),
        (over_x, 0, over_y), (over_y, 1, over_x),
    )
    arrivals = ((over_x, 0), (over_x, 1), (over_y, 1), (over_y, 0), (across, 0), (across, 1))

    def relay(blocks, sends, receives, j, section):
        owner, half, target = steps[j]
        part = blocks.at[owner, half * 32 : half * 32 + 32]
        return remote(part, part, sends.at[j], receives.at[j], place(section, z, target))

    def relay_landed(blocks, receives, j):
        owner, half = arrivals[j]
        landed(blocks.at[owner, half * 32 : half * 32 + 32], receives.at[j])

    def forward(layer, j):
        return relay(wo.at[layer], f_s.at[layer], f_r.at[layer], j, 1)

    def forward_landed(layer, j):
        relay_landed(wo.at[layer], f_r.at[layer], j)

    def pass_on(layer):
        forward_landed(layer, 0)
        forward(layer, 4).start()
        forward_landed(layer, 2)
        forward(layer, 5).start()

    def shards_landed(layer):
        for zz in range(count):
            dst = wo.at[layer, c, :, zz * shard : (zz + 1) * shard]
            if layer == 0:
                landed(dst, w_r.at[layer, zz])
            else:
                @pl.when(z != zz)
                def _():
                    landed(dst, w_r.at[layer, zz])

    def forwards_landed(layer):
        for j in (1, 3, 4, 5):
            forward_landed(layer, j)

    def text_mask(start, rows):
        i = lax.broadcasted_iota(jnp.int32, (rows, 1), 0) + start
        return (i // 16) * 64 + z * 16 + i % 16 < TEXT

    def norm16(values):
        values = values.astype(jnp.float32)
        centered = values - jnp.mean(values, axis=-1, keepdims=True)
        return centered * lax.rsqrt(jnp.mean(centered * centered, axis=-1, keepdims=True) + 1e-05)

    def out_projection(layer, prev, gates):
        for h in range(count):
            landed(att_in.at[layer, h], a_r.at[layer, h])
        rows = [att_in[layer, h].reshape(64, 128)[:, HD:] for h in range(count)]
        joined = jnp.concatenate(rows, axis=1)
        text = text_mask(0, 64)
        for part in range(4):
            cols = slice(part * (width // 4), (part + 1) * (width // 4))
            weight = wo[layer, :, :, cols].reshape(4 * HD, width // 4)
            update = jnp.dot(joined, weight, preferred_element_type=jnp.float32)
            gate = jnp.where(text, gates[5:6, cols], gates[2:3, cols])
            x_buf[:, cols] = (prev[:, cols].astype(jnp.float32) + gate * update).astype(jnp.bfloat16)

    mod_copy = remote(mod, mod0, m_s, m_r, place(1, z, c))

    def mix_rows(p, carry):
        rows = pl.ds(pl.multiple_of(p * 16, 16), 16)
        text = text_mask(p * 16, 16)
        normed = norm16(x_buf[rows, :])
        scale = jnp.where(text, mod[4:5, :], mod[1:2, :])
        shift = jnp.where(text, mod[3:4, :], mod[0:1, :])
        mix[c, rows, :] = (normed * (1.0 + scale) + shift).astype(jnp.bfloat16)
        return carry

    def gather(j):
        return relay(mix, g_s, g_r, j, sec)

    local[0].wait()
    local[1].wait()

    @pl.when(sec == 0)
    def _():
        lax.fori_loop(0, 4, mix_rows, 0)

    pl.semaphore_wait(barrier, everyone - 1)
    local[2].wait()

    @pl.when(sec == 0)
    def _():
        for j in (0, 2, 1, 3):
            gather(j).start()
        mod_copy.start()
        for k in range(count):
            shard_copy(0, k).start()

    @pl.when(sec == 1)
    def _():
        for k in range(1, count):
            shard_copy(1, k).start()
        wo[1, c, :, own_cols] = wout[...]
        shards_landed(0)
        pl.semaphore_wait(go, 1)
        for j in (0, 2, 1, 3):
            forward(0, j).start()
        pass_on(0)
        shards_landed(1)
        mod_copy.wait_recv()
        forwards_landed(0)
        out_projection(0, x_buf, mod0)
        lax.fori_loop(0, 2, mix_rows, 0)
        gather(0).start()
        lax.fori_loop(2, 4, mix_rows, 0)
        for j in (2, 1, 3):
            gather(j).start()

    for copy in local[3:]:
        copy.wait()

    contract = (((1,), (1,)), ((), ()))
    lane = lax.broadcasted_iota(jnp.int32, (1, 128), 1)
    head = lane < HD
    low = (lane // 32) % 2 == 0

    def prepare(values, cos_table, sin_table):
        mean = jnp.sum(jnp.where(head, values, 0.0), axis=-1, keepdims=True) * (1.0 / HD)
        centered = values - mean
        square = jnp.where(head, centered * centered, 0.0)
        scale = lax.rsqrt(jnp.sum(square, axis=-1, keepdims=True) * (1.0 / HD) + 1e-06)
        normed = jnp.where(head, centered * scale, values)
        swapped = jnp.where(low, pltpu.roll(normed, 96, 1), pltpu.roll(normed, 32, 1))
        return (normed * cos_table + swapped * sin_table).astype(jnp.bfloat16).reshape(4, 16, 128)

    def qkv_copy(s):
        return remote(
            qkv_out.at[s], qkv_in.at[:, z], q_s.at[s], q_r.at[z], place(sec, s, c)
        )

    for k, s in enumerate((c, over_x, over_y, across)):
        if k == 1:
            relay_landed(mix, g_r, 0)
            gather(4).start()
            relay_landed(mix, g_r, 2)
            gather(5).start()
            relay_landed(mix, g_r, 1)
        if k == 2:
            relay_landed(mix, g_r, 3)
        if k == 3:
            relay_landed(mix, g_r, 4)
            relay_landed(mix, g_r, 5)
        projected = lax.dot_general(mix[s], wqkv[...], contract, preferred_element_type=jnp.float32)
        cos_table = cos_t[s // 2]
        sin_table = sin_t[s // 2]
        kv = prepare(projected[:, HD:], cos_table, sin_table)
        qq = prepare(projected[:, :128], cos_table, sin_table)

        qkv_out[s, :, :, :128] = kv
        qkv_out[s, :, :, 128:] = qq

        @pl.when(s != z)
        def _():
            qkv_copy(s).start()

    @pl.when(sec == 0)
    def _():
        pl.semaphore_signal(
            go, inc=1, device_id=place(1, z, c), device_id_type=pl.DeviceIdType.MESH
        )

    @pl.when(sec == 1)
    def _():
        for j in (0, 2, 1, 3):
            forward(1, j).start()

    qkv_in[:, z] = qkv_out[z]
    for k in range(1, count):
        zz = lax.rem(z + k, 4)
        landed(qkv_in.at[:, zz], q_r.at[zz])

    @pl.when(sec == 1)
    def _():
        pass_on(1)

    fresh = qkv_in[:, :, :, :128].reshape(256, 128)
    query = qkv_in[:, :, :, 128:].reshape(256, 128)[:, :HD]
    cache_out[...] = fresh
    old = stale[...]
    key_row = lax.broadcasted_iota(jnp.int32, (1, 256), 1)
    limit = jnp.where(key_row < TEXT, texts[z], TEXT + videos[z // 2])
    bias = jnp.where(key_row < limit, 0.0, -jnp.inf)
    fresh_scores = lax.dot_general(query, fresh[:, :HD], contract, preferred_element_type=jnp.float32)
    old_scores = lax.dot_general(query, old[:, :HD], contract, preferred_element_type=jnp.float32)
    query_patch = lax.broadcasted_iota(jnp.int32, (256, 256), 0) // 64
    key_patch = lax.broadcasted_iota(jnp.int32, (256, 256), 1) // 64
    is_fresh = key_patch <= query_patch
    scores = jnp.where(is_fresh, fresh_scores, old_scores) * (HD ** -0.5) + bias
    weights = jnp.exp(scores - jnp.max(scores, axis=1, keepdims=True))
    total = jnp.sum(weights, axis=1, keepdims=True)
    combined = jnp.dot(
        jnp.where(is_fresh, weights, 0.0).astype(jnp.bfloat16), fresh,
        preferred_element_type=jnp.float32,
    ) + jnp.dot(
        jnp.where(is_fresh, 0.0, weights).astype(jnp.bfloat16), old,
        preferred_element_type=jnp.float32,
    )
    att_out[...] = (combined / total).astype(jnp.bfloat16).reshape(4, 4, 16, 128)

    def att_copy(zz):
        return remote(
            att_out.at[:, zz], att_in.at[sec, c], a_s.at[zz], a_r.at[sec, c], place(1, zz, z)
        )

    def own_copy(zz):
        return pltpu.make_async_copy(att_out.at[:, zz], att_in.at[1, c], a_r.at[1, c])

    for zz in range(count):
        stays = jnp.logical_and(sec == 1, jnp.logical_and(z == zz, c == z))

        @pl.when(stays)
        def _():
            own_copy(zz).start()

        @pl.when(jnp.logical_not(stays))
        def _():
            att_copy(zz).start()

    def pred_copy(k):
        return remote(
            pred, pred_in.at[c % 2], p_s.at[k], p_r.at[c % 2],
            place(c // 2, z, lax.rem(c + k, 4)),
        )

    @pl.when(sec == 1)
    def _():
        forwards_landed(1)
        out_projection(1, x_buf, mod)

        def last_rows(p, carry):
            rows = pl.ds(pl.multiple_of(p * 16, 16), 16)
            normed = norm16(x_buf[rows, :])
            fin[rows, :] = (normed * (1.0 + omod[1:2, :]) + omod[0:1, :]).astype(jnp.bfloat16)
            return carry

        lax.fori_loop(0, 4, last_rows, 0)
        pred[...] = lax.dot_general(
            fin[...], proj[...], contract, preferred_element_type=jnp.float32
        )

        @pl.when(c // 2 == 0)
        def _():
            pred_copy(0).start()

        @pl.when(c // 2 == 1)
        def _():
            pltpu.make_async_copy(pred, pred_in.at[c % 2], p_r.at[c % 2]).start()

        for k in range(1, count):
            pred_copy(k).start()

    for half in range(2):
        landed(pred_in.at[half], p_r.at[half])
    first = pred_in[0]
    guided = first + coef[0, 2] * (pred_in[1] - first)
    lat_out[...] = coef[0, 0] * lat[...] + coef[0, 1] * guided

    @pl.when(sec == 0)
    def _():
        mod_copy.wait_send()
        for k in range(count):
            shard_copy(0, k).wait_send()

    @pl.when(sec == 1)
    def _():
        for k in range(1, count):
            shard_copy(1, k).wait_send()
            pred_copy(k).wait_send()
        for j in range(6):
            forward(0, j).wait_send()
            forward(1, j).wait_send()

        @pl.when(c // 2 == 0)
        def _():
            pred_copy(0).wait_send()

    for j in range(6):
        gather(j).wait_send()
    for k in range(1, count):
        qkv_copy(lax.rem(z + k, 4)).wait_send()
    for zz in range(count):
        stays = jnp.logical_and(sec == 1, jnp.logical_and(z == zz, c == z))

        @pl.when(jnp.logical_not(stays))
        def _():
            att_copy(zz).wait_send()


def fused(
    hidden_states, latent, stale_cache, qkv_weight, out_weight, modulation, out_modulation,
    proj_weight, solver_coef, video_len, text_len, positions,
):
    z = lax.axis_index("seq")
    width = hidden_states.shape[3]
    wqkv = qkv_weight[0].transpose(1, 2, 0).reshape(3 * HD, width)
    wout = out_weight[0].T
    rows = jnp.arange(64)
    row_place = (rows // 16) * 64 + z * 16 + rows % 16
    places = positions.reshape(3, 2, 64).astype(jnp.float32)
    angles = rope_angles(places, HD)
    angles = jnp.where((row_place < TEXT)[None, :, None], 0.0, angles)
    cos, sin = jnp.cos(angles), jnp.sin(angles)
    rest = jnp.zeros((2, 64, HD), jnp.float32)
    cos_t = jnp.concatenate([cos, cos, rest + 1.0], axis=-1)
    sin_t = jnp.concatenate([-sin, sin, rest], axis=-1)
    vmem = pl.BlockSpec(memory_space=pltpu.VMEM)
    far = pl.BlockSpec(memory_space=pl.ANY)
    smem = pl.BlockSpec(memory_space=pltpu.SMEM)
    dma = pltpu.SemaphoreType.DMA
    bf16, f32 = jnp.bfloat16, jnp.float32
    new_latent, new_cache = pl.pallas_call(
        fused_kernel,
        out_shape=(
            jax.ShapeDtypeStruct((64, 64), f32),
            jax.ShapeDtypeStruct((256, 128), bf16),
        ),
        in_specs=[far] * 8 + [smem] * 3 + [vmem] * 2,
        out_specs=(vmem, vmem),
        scratch_shapes=[
            pltpu.VMEM((64, width), bf16),
            pltpu.VMEM((64, 64), f32),
            pltpu.VMEM((256, 128), bf16),
            pltpu.VMEM((3 * HD, width), bf16),
            pltpu.VMEM(wout.shape, bf16),
            pltpu.VMEM((6, width), f32),
            pltpu.VMEM((2, width), f32),
            pltpu.VMEM((64, width), bf16),
            dma((8,)),
            pltpu.VMEM((4, 64, width), bf16),
            pltpu.VMEM((4, 4, 16, 256), bf16),
            pltpu.VMEM((4, 4, 16, 256), bf16),
            pltpu.VMEM((4, 4, 16, 128), bf16),
            pltpu.VMEM((2, 4, 4, 16, 128), bf16),
            pltpu.VMEM((2, 4, HD, width), bf16),
            pltpu.VMEM((6, width), f32),
            pltpu.VMEM((64, width), bf16),
            pltpu.VMEM((64, 64), f32),
            pltpu.VMEM((2, 64, 64), f32),
            dma((6,)), dma((6,)), dma((4,)), dma((4,)), dma((4,)), dma((2, 4)),
            dma((4,)), dma((2, 4)), dma((2, 6)), dma((2, 6)), dma, dma, dma((4,)), dma((2,)),
            pltpu.SemaphoreType.REGULAR,
        ],
        compiler_params=pltpu.CompilerParams(
            collective_id=0, has_side_effects=True, vmem_limit_bytes=64 * 1024 * 1024
        ),
    )(
        hidden_states.reshape(64, width), latent.reshape(64, 64), stale_cache[0, 0, 0], wqkv, wout,
        modulation[0], out_modulation, proj_weight.T, solver_coef, text_len, video_len,
        cos_t, sin_t,
    )
    return new_latent.reshape(latent.shape), new_cache.reshape(stale_cache.shape)


def per_device(*args):
    hidden_states, latent, stale_cache, qkv_weight = args[:4]
    sizes = tuple(lax.axis_size(axis) for axis in ("section", "seq", "cfg"))
    small = (
        sizes == (2, 4, 4)
        and hidden_states.shape[:3] == (1, 4, 16)
        and latent.shape == (1, 4, 16, 64)
        and stale_cache.shape == (1, 1, 1, 256, 128)
        and qkv_weight.shape[3] == HD
    )
    return fused(*args) if small else general(*args)


def solution(mesh):
    return jax.shard_map(
        per_device,
        mesh=mesh,
        in_specs=(
            P("cfg", None, "seq", None),
            P("section", None, "seq", None),
            P("section", "cfg", "seq", None, None),
            P("section", None, None, "cfg"),
            P("section", "seq", "cfg"),
            P("section", None, None),
            P(),
            P(),
            P("section", None),
            P(),
            P(),
            P(None, None, None, "seq"),
        ),
        out_specs=(P("section", None, "seq", None), P("section", "cfg", "seq", None, None)),
        check_vma=False,
    )
```
